768 devices in a mesh: rep: 12 (over z), fsdp: 32 (over x, y), sub: 2 (over core).
Axes of the slice: x: 4, y: 8, z: 12, core: 2. Of those that a mesh axis runs over, the one named last changes fastest.
Arguments:
- grads: bfloat16 [12, 64, 3584, 288], P('rep', None, ('fsdp', 'sub')), may hold values from -6 to 6
- momentum: bfloat16 [64, 3584, 288], P(None, ('fsdp', 'sub')), may hold values from -18 to 18
- owner: int32 [64], replicated, may hold values from 0 to 63, each once
Outputs:
- new_momentum: bfloat16 [64, 3584, 288], P(None, ('fsdp', 'sub'))
- update: bfloat16 [64, 3584, 288], P(None, ('fsdp', 'sub'))
- owned_update: bfloat16 [64, 3584, 288], P(('fsdp', 'sub'))
The draws below stay inside these ranges and needn't reach their ends.
Inputs may be any that keep to these rules, and one draw needn't show every extreme that they name: owner is a permutation: each group device owns exactly one matrix.
All inputs are finite; a program needn't handle non-finite values.
Results may differ from the reference program's by a relative error of at most 0.034.
Values may be sent and summed in bfloat16 or wider, within the bound.
No kernel may reach another device: no remote copies, remote signals or barrier semaphores. Data moves between devices by JAX's collectives and lax.ppermute only.
A program may use at most 64 MiB of HBM per device.

```python
import jax
import jax.numpy as jnp
from jax import lax

D = 3584
RANK = 288
ITERS = 3
MATRICES = 64
REPLICAS = 12


def shard_levels(key, dims, split, low, top_value):
    def one(position, shards_of):
        steps = jax.random.uniform(jax.random.fold_in(jax.random.fold_in(key, 6), position), (shards_of,), jnp.float32, low / len(split), top_value / len(split))
        return jnp.repeat(jnp.exp(steps), dims[position] // shards_of).reshape((-1,) + (1,) * (len(dims) - position - 1))

    factor_of = one(*split[0])
    for cut in split[1:]:
        factor_of = factor_of * one(*cut)
    return factor_of


def centred(key, shape, spread, most, split=(), held_as=jnp.bfloat16):
    factor_of = shard_levels(key, shape, split, -0.22, 0.18) if split else 1.0
    result = jax.random.normal(key, shape, jnp.float32) * spread * factor_of
    return jnp.minimum(jnp.maximum(result, -most), most).astype(held_as)


def setup_inputs(seed: int = 0) -> dict:
    key_of = jax.random.split(jax.random.key(seed), 4)
    return {
        "grads": centred(key_of[0], (REPLICAS, MATRICES, D, RANK), 1.0, 6.0, ((0, 12), (2, 64))),
        "momentum": centred(key_of[1], (MATRICES, D, RANK), 3.0, 18.0, ((1, 64),)),
        "owner": jax.random.permutation(key_of[2], MATRICES).astype(jnp.int32),
    }


def orthogonal(ahead):
    whole = ahead.astype(jnp.float32)
    scale = jnp.sqrt(jnp.sum(whole * whole)) + 1e-07
    ycur = (whole / scale).astype(jnp.bfloat16)
    for step in range(ITERS):
        gram = jnp.dot(ycur.T, ycur, preferred_element_type=jnp.float32).astype(jnp.bfloat16)
        square = jnp.dot(gram, gram, preferred_element_type=jnp.float32)
        mixed = (-4.775 * gram.astype(jnp.float32) + 2.0315 * square).astype(jnp.bfloat16)
        ycur = (3.4445 * ycur.astype(jnp.float32) + jnp.dot(ycur, mixed, preferred_element_type=jnp.float32)).astype(jnp.bfloat16)
    factor = 0.2 * max(D, RANK) ** 0.5
    return (factor * ycur.astype(jnp.float32)).astype(jnp.bfloat16)

def reference(grads, momentum, owner):

    def single(index):
        total = lax.optimization_barrier(jnp.sum(grads[:, index].astype(jnp.float32), axis=0))
        moment = 0.95 * momentum[index].astype(jnp.float32) + total
        ahead = (total + 0.95 * moment).astype(jnp.bfloat16)
        return (moment.astype(jnp.bfloat16), orthogonal(ahead))
    new_momentum, update = lax.map(single, jnp.arange(MATRICES, dtype=jnp.int32))
    inverse = jnp.argsort(owner).astype(jnp.int32)
    owned_update = jnp.take(update, inverse, axis=0)
    return (new_momentum, update, owned_update)
```

```python
import functools

import jax
import jax.numpy as jnp
from jax import lax
from jax.experimental import pallas as pl
from jax.experimental.pallas import tpu as pltpu
from jax.sharding import PartitionSpec as P

ITERS = 3
GROUP = ("fsdp", "sub")
F32 = jnp.float32
BF16 = jnp.bfloat16
SLOTS_PER_STEP = 16
VMEM_LIMIT = 56 * 1024 * 1024
SMEM = pl.BlockSpec(memory_space=pltpu.SMEM)
VMEM = pl.BlockSpec(memory_space=pltpu.VMEM)


def call(kernel, out_shape, n_in, scalars=0, scratch=(), flops=0, moved=4 << 20):
    several = isinstance(out_shape, (list, tuple))
    return pl.pallas_call(
        kernel,
        out_shape=out_shape,
        in_specs=[SMEM] * scalars + [VMEM] * n_in,
        out_specs=[VMEM] * len(out_shape) if several else VMEM,
        scratch_shapes=list(scratch),
        compiler_params=pltpu.CompilerParams(vmem_limit_bytes=VMEM_LIMIT),
        cost_estimate=pl.CostEstimate(flops=flops, bytes_accessed=moved, transcendentals=0),
    )


def shape(dims, dtype=BF16):
    return jax.ShapeDtypeStruct(dims, dtype)


def each(count, one, together=8):
    together = min(together, count)

    def several(k, carry):
        for i in range(together):
            one(k * together + i)
        return carry

    lax.fori_loop(0, count // together, several, 0)


def select_rows(first, count, width):
    row = lax.broadcasted_iota(jnp.int32, (count, width), 0)
    col = lax.broadcasted_iota(jnp.int32, (count, width), 1)
    return (col == row + first).astype(BF16)


def turn_kernel(owner_ref, first_ref, x_ref, out_ref, by_slot):
    count, rows, cols = x_ref.shape

    def place(j):
        by_slot[owner_ref[j]] = x_ref[j].astype(F32)

    each(count, place)
    pick = select_rows(first_ref[0], out_ref.shape[0], cols)
    step = SLOTS_PER_STEP
    for k in range(count // step):
        part = by_slot[k * step : (k + 1) * step].reshape(step * rows, cols).astype(BF16)
        turned = lax.dot_general(pick, part, (((1,), (1,)), ((), ())), preferred_element_type=F32)
        out_ref[:, k * step * rows : (k + 1) * step * rows] = turned.astype(BF16)


def turn(owner, first, x, picked):
    count, rows, cols = x.shape
    return call(
        turn_kernel,
        shape((picked, count * rows)),
        1,
        scalars=2,
        scratch=[pltpu.VMEM(x.shape, F32)],
        flops=2 * count * rows * cols * picked,
    )(owner, first, x)


def moment_kernel(count, total_ref, momentum_ref, new_ref, out_ref):
    total = total_ref[...].astype(F32)
    moment = 0.95 * momentum_ref[...].astype(F32) + total
    new_ref[...] = moment.astype(BF16)
    ahead = total + 0.95 * moment
    rows = total.shape[1] // count
    for s in range(count):
        block = ahead[:, s * rows : (s + 1) * rows].astype(BF16)
        out_ref[s, :, :rows] = block[:16]
        out_ref[s, :8, 64 : 64 + rows] = block[16:]


def join_kernel(x_ref, left_ref, right_ref, whole):
    count = x_ref.shape[0]
    half = left_ref.shape[1]
    rows = 2 * half // count
    for s in range(count):
        block = x_ref[s].astype(F32)
        whole[:16, s * rows : (s + 1) * rows] = block[:, :rows]
        whole[16:, s * rows : (s + 1) * rows] = block[:8, 64 : 64 + rows]
    left_ref[...] = whole[:, :half].astype(BF16)
    right_ref[...] = whole[:, half:].astype(BF16)


def untransposed(part):
    eye = select_rows(0, part.shape[0], part.shape[0])
    return lax.dot_general(part, eye, (((0,), (0,)), ((), ())), preferred_element_type=F32)


def orthogonal_kernel(count, factor, left_ref, right_ref, owned_ref, packed_ref, y_ref):
    cols, half = left_ref.shape
    squares = jnp.zeros((1, 1), F32)
    for ref in (left_ref, right_ref):
        value = ref[...].astype(F32)
        squares += jnp.sum(value * value, keepdims=True)
    scale = jnp.sqrt(squares) + 1e-07
    for k, ref in enumerate((left_ref, right_ref)):
        y_ref[:, k * half : (k + 1) * half] = (ref[...].astype(F32) / scale).astype(BF16)
    length = 2 * half
    rows = length // count
    step = SLOTS_PER_STEP
    for it in range(ITERS):
        y = y_ref[...]
        gram = lax.dot_general(y, y, (((1,), (1,)), ((), ())), preferred_element_type=F32).astype(BF16)
        square = jnp.dot(gram, gram, preferred_element_type=F32)
        mixed = (-4.775 * gram.astype(F32) + 2.0315 * square).astype(BF16)
        for k in range(count // step):
            at = slice(k * step * rows, (k + 1) * step * rows)
            old = y_ref[:, at]
            new = (3.4445 * old.astype(F32) + jnp.dot(mixed, old, preferred_element_type=F32)).astype(BF16)
            if it < ITERS - 1:
                y_ref[:, at] = new
            else:
                new = (factor * new.astype(F32)).astype(BF16)
                owned_ref[:, at] = new
                update = untransposed(new).reshape(step, rows, cols)
                main = update[:, :, :256]
                tail = jnp.concatenate(
                    [update[:, 8 * j : 8 * j + 8, 256:] for j in range(rows // 8)]
                    + [jnp.zeros((step, 8, 32), F32)],
                    axis=2,
                )
                packed_ref[k * step : (k + 1) * step] = jnp.concatenate([main, tail], axis=1).astype(BF16)


def unpack_kernel(owner_ref, packed_ref, out_ref):
    count, rows, cols = out_ref.shape

    def one(j):
        block = packed_ref[owner_ref[j]].astype(F32)
        tail = jnp.concatenate([block[rows:, 32 * k : 32 * k + 32] for k in range(rows // 8)], axis=0)
        out_ref[j] = jnp.concatenate([block[:rows], tail], axis=1).astype(BF16)

    each(count, one)


def unturn_kernel(owner_ref, x_ref, out_ref, by_slot):
    count, rows, cols = out_ref.shape
    step = SLOTS_PER_STEP
    for k in range(count // step):
        part = untransposed(x_ref[:, k * step * rows : (k + 1) * step * rows])
        by_slot[k * step : (k + 1) * step] = part.reshape(step, rows, cols)

    def one(j):
        out_ref[j] = by_slot[owner_ref[j]].astype(BF16)

    each(count, one)


def body(grads, momentum, owner):
    _, count, rows, cols = grads.shape
    reps = lax.axis_size("rep")
    share = cols // reps
    length = count * rows
    half = length // 2
    zero = jnp.zeros((1,), jnp.int32)
    first = (lax.axis_index("rep") * share).astype(jnp.int32).reshape(1)
    turned = turn(owner, zero, grads[0], cols)
    total = lax.psum_scatter(turned, "rep", scatter_dimension=0, tiled=True)
    mine = turn(owner, first, momentum, share)
    new_share, outgoing = call(
        functools.partial(moment_kernel, count), [shape((share, length)), shape((count, 16, 128))], 2
    )(total, mine)
    new_turned = lax.all_gather(new_share, "rep", axis=0, tiled=True)
    arrived = lax.all_to_all(outgoing, GROUP, split_axis=0, concat_axis=0, tiled=True)
    left, right = call(
        join_kernel, [shape((share, half))] * 2, 1, scratch=[pltpu.VMEM((share, length), F32)]
    )(arrived)
    left = lax.all_gather(left, "rep", axis=0, tiled=True)
    right = lax.all_gather(right, "rep", axis=0, tiled=True)
    factor = 0.2 * max(length, cols) ** 0.5
    owned, packed = call(
        functools.partial(orthogonal_kernel, count, factor),
        [shape((cols, length)), shape((count, rows + 8, 256))],
        2,
        scratch=[pltpu.VMEM((cols, length), BF16)],
        flops=4 * ITERS * length * cols * cols,
    )(left, right)
    packed, new_turned = lax.optimization_barrier((packed, new_turned))
    returned = lax.all_to_all(packed, GROUP, split_axis=0, concat_axis=0, tiled=True)
    new_momentum = call(
        unturn_kernel,
        shape((count, rows, cols)),
        1,
        scalars=1,
        scratch=[pltpu.VMEM((count, rows, cols), F32)],
        flops=2 * length * cols * cols,
    )(owner, new_turned)
    update = call(unpack_kernel, shape((count, rows, cols)), 1, scalars=1)(owner, returned)
    return (new_momentum, update, owned.T[None])


def solution(mesh):
    placed = (P("rep", None, GROUP, None), P(None, GROUP, None), P())
    return jax.shard_map(
        body,
        mesh=mesh,
        in_specs=placed,
        out_specs=(P(None, GROUP, None), P(None, GROUP, None), P(GROUP, None, None)),
        check_vma=False,
    )
```

```python
import functools

import jax
import jax.numpy as jnp
from jax import lax
from jax.experimental import pallas as pl
from jax.experimental.pallas import tpu as pltpu
from jax.sharding import Mesh, PartitionSpec as P

ITERS = 3
GROUP = ("fsdp", "sub")
F32 = jnp.float32
BF16 = jnp.bfloat16
SLOTS_PER_STEP = 16
LANES = 128
SPARE = 16
NEAR = 3
VMEM_LIMIT = 32 * 1024 * 1024
SMEM = pl.BlockSpec(memory_space=pltpu.SMEM)
VMEM = pl.BlockSpec(memory_space=pltpu.VMEM)


def call(kernel, out_shape, n_in, scalars=0, scratch=(), flops=0, moved=4 << 20):
    several = isinstance(out_shape, (list, tuple))
    return pl.pallas_call(
        kernel,
        out_shape=out_shape,
        in_specs=[SMEM] * scalars + [VMEM] * n_in,
        out_specs=[VMEM] * len(out_shape) if several else VMEM,
        scratch_shapes=list(scratch),
        compiler_params=pltpu.CompilerParams(vmem_limit_bytes=VMEM_LIMIT),
        cost_estimate=pl.CostEstimate(flops=flops, bytes_accessed=moved, transcendentals=0),
    )


def shape(dims, dtype=BF16):
    return jax.ShapeDtypeStruct(dims, dtype)


def each(count, one, together=8):
    together = min(together, count)

    def several(k, carry):
        for i in range(together):
            one(k * together + i)
        return carry

    lax.fori_loop(0, count // together, several, 0)


def select_rows(first, count, width):
    row = lax.broadcasted_iota(jnp.int32, (count, width), 0)
    col = lax.broadcasted_iota(jnp.int32, (count, width), 1)
    return (col == row + first).astype(BF16)


def select_shares(share, width):
    row = lax.broadcasted_iota(jnp.int32, (width, width), 0)
    col = lax.broadcasted_iota(jnp.int32, (width, width), 1)
    reps = width // share
    picked = row
    for r in range(reps):
        hi, lo = r // NEAR, r % NEAR
        start = lo * (width // NEAR) + hi * share
        inside = (row >= r * share) & (row < (r + 1) * share)
        picked = jnp.where(inside, row + (start - r * share), picked)
    return (col == picked).astype(BF16)


def place_by_owner(owner_ref, x_ref, by_slot):
    def place(j):
        by_slot[owner_ref[j]] = x_ref[j].astype(F32)

    each(x_ref.shape[0], place)


def turned_part(pick, by_slot, k, step):
    _, rows, cols = by_slot.shape
    part = by_slot[k * step : (k + 1) * step].reshape(step * rows, cols).astype(BF16)
    return lax.dot_general(pick, part, (((1,), (1,)), ((), ())), preferred_element_type=F32)


def turn_grads_kernel(share, x_ref_owner, x_ref, out_ref, by_slot):
    count, rows, cols = x_ref.shape
    place_by_owner(x_ref_owner, x_ref, by_slot)
    pick = select_shares(share, cols)
    step = min(2 * SLOTS_PER_STEP, count)
    tiles = step * rows // LANES
    held = share * count * rows // LANES
    out_ref[...] = jnp.zeros(out_ref.shape, BF16)
    for k in range(count // step):
        turned = turned_part(pick, by_slot, k, step)
        for r in range(cols // share):
            mine = turned[r * share : (r + 1) * share]
            block = jnp.concatenate([mine[:, t * LANES : (t + 1) * LANES] for t in range(tiles)], axis=0)
            first = r * (held + SPARE) + k * tiles * share
            out_ref[first : first + tiles * share] = block.astype(BF16)


def turn_share_kernel(owner_ref, first_ref, x_ref, out_ref, by_slot):
    count, rows, cols = x_ref.shape
    place_by_owner(owner_ref, x_ref, by_slot)
    pick = select_rows(first_ref[0], out_ref.shape[0], cols)
    step = SLOTS_PER_STEP
    for k in range(count // step):
        out_ref[:, k * step * rows : (k + 1) * step * rows] = turned_part(pick, by_slot, k, step).astype(BF16)


def moment_kernel(count, total_ref, momentum_ref, new_ref, out_ref):
    rows_of = momentum_ref.shape[0]
    held = total_ref[...].astype(F32)
    total = jnp.concatenate([held[t : t + rows_of] for t in range(0, held.shape[0], rows_of)], axis=1)
    moment = 0.95 * momentum_ref[...].astype(F32) + total
    new_ref[...] = moment.astype(BF16)
    ahead = total + 0.95 * moment
    rows = total.shape[1] // count
    for s in range(count):
        block = ahead[:, s * rows : (s + 1) * rows].astype(BF16)
        out_ref[s, :, :rows] = block[:16]
        out_ref[s, :8, 64 : 64 + rows] = block[16:]


def join_kernel(x_ref, out_ref, whole):
    count = x_ref.shape[0]
    rows = out_ref.shape[1] // count
    for s in range(count):
        block = x_ref[s].astype(F32)
        whole[:16, s * rows : (s + 1) * rows] = block[:, :rows]
        whole[16:, s * rows : (s + 1) * rows] = block[:8, 64 : 64 + rows]
    out_ref[...] = whole[...].astype(BF16)


def untransposed(part, eye):
    return lax.dot_general(part, eye, (((0,), (0,)), ((), ())), preferred_element_type=F32)


def orthogonal_kernel(count, factor, third_ref, own_ref, before_ref, after_ref, owned_ref, packed_ref, y_ref):
    third, length = own_ref.shape
    lo = third_ref[0]

    def of_third(which):
        return pl.ds(pl.multiple_of(lax.rem(which, NEAR) * third, third), third)

    y_ref[of_third(lo), :] = own_ref[...]
    y_ref[of_third(lo + NEAR - 1), :] = before_ref[...]
    y_ref[of_third(lo + 1), :] = after_ref[...]
    squares = jnp.zeros((1, 1), F32)
    for k in range(NEAR):
        value = y_ref[k * third : (k + 1) * third, :].astype(F32)
        squares += jnp.sum(value * value, keepdims=True)
    inverse = 1.0 / (jnp.sqrt(squares) + 1e-07)
    for k in range(NEAR):
        at = slice(k * third, (k + 1) * third)
        y_ref[at, :] = (y_ref[at, :].astype(F32) * inverse).astype(BF16)
    rows = length // count
    step = SLOTS_PER_STEP
    eye = select_rows(0, third, third)
    for it in range(ITERS):
        y = y_ref[...]
        gram = lax.dot_general(y, y, (((1,), (1,)), ((), ())), preferred_element_type=F32).astype(BF16)
        square = jnp.dot(gram, gram, preferred_element_type=F32)
        mixed = (-4.775 * gram.astype(F32) + 2.0315 * square).astype(BF16)
        for k in range(count // step):
            at = slice(k * step * rows, (k + 1) * step * rows)
            old = y_ref[:, at]
            new = (3.4445 * old.astype(F32) + jnp.dot(mixed, old, preferred_element_type=F32)).astype(BF16)
            if it < ITERS - 1:
                y_ref[:, at] = new
            else:
                owned_ref[:, at] = (factor * new.astype(F32)).astype(BF16)
                update = untransposed(owned_ref[of_third(lo), at], eye).reshape(step, rows, third)
                top = rows - 8
                low = [update[:, top:, 32 * j : 32 * j + 32] for j in range(third // 32)]
                low.append(jnp.zeros((step, top - 8 * len(low), 32), F32))
                block = jnp.concatenate([update[:, :top], jnp.concatenate(low, axis=1)], axis=2)
                packed_ref[k * step : (k + 1) * step] = block.astype(BF16)


def unpack_kernel(owner_ref, third_ref, own_ref, before_ref, after_ref, out_ref):
    count, rows, cols = out_ref.shape
    third = cols // NEAR
    top = rows - 8

    def columns(block):
        low = [block[8 * k : 8 * k + 8, third:] for k in range(third // 32)]
        return jnp.concatenate([block[:top, :third], jnp.concatenate(low, axis=1)], axis=0)

    for lo in range(NEAR):

        @pl.when(third_ref[0] == lo)
        def _():
            refs = [None] * NEAR
            refs[lo], refs[(lo + NEAR - 1) % NEAR], refs[(lo + 1) % NEAR] = own_ref, before_ref, after_ref

            def one(j):
                slot = owner_ref[j]
                parts = [columns(ref[slot].astype(F32)) for ref in refs]
                out_ref[j] = jnp.concatenate(parts, axis=1).astype(BF16)

            each(count, one, 4)


def unturn_kernel(share, owner_ref, x_ref, out_ref, by_slot):
    count, rows, cols = out_ref.shape
    step = SLOTS_PER_STEP
    pick = select_shares(share, cols)
    for k in range(count // step):
        part = untransposed(x_ref[:, k * step * rows : (k + 1) * step * rows], pick)
        by_slot[k * step : (k + 1) * step] = part.reshape(step, rows, cols)

    def one(j):
        out_ref[j] = by_slot[owner_ref[j]].astype(BF16)

    each(count, one)


def with_neighbours(part):
    reps = lax.axis_size("hi") * lax.axis_size("lo")
    before = lax.ppermute(part, ("hi", "lo"), [(r, (r + 1) % reps) for r in range(reps)])
    after = lax.ppermute(part, ("hi", "lo"), [((r + 1) % reps, r) for r in range(reps)])
    return part, before, after


def body(grads, momentum, owner):
    _, count, rows, cols = grads.shape
    reps = lax.axis_size("hi") * lax.axis_size("lo")
    share = cols // reps
    third = cols // NEAR
    length = count * rows
    hi, lo = lax.axis_index("hi").astype(jnp.int32), lax.axis_index("lo").astype(jnp.int32)
    first = (lo * third + hi * share).reshape(1)
    lo = lo.reshape(1)
    by_slot = [pltpu.VMEM((count, rows, cols), F32)]
    held = share * length // LANES
    turned = call(
        functools.partial(turn_grads_kernel, share),
        shape((reps * (held + SPARE - 1), LANES)),
        1,
        scalars=1,
        scratch=by_slot,
        flops=2 * length * cols * cols,
    )(owner, grads[0])
    total = lax.psum_scatter(turned, ("hi", "lo"), scatter_dimension=0, tiled=True)
    total = lax.optimization_barrier(total)
    total = lax.dynamic_slice(total, (lax.axis_index(("hi", "lo")), 0), (held, LANES))
    mine = call(
        turn_share_kernel, shape((share, length)), 1, scalars=2, scratch=by_slot, flops=2 * length * cols * share
    )(owner, first, momentum)
    new_share, outgoing = call(
        functools.partial(moment_kernel, count), [shape((share, length)), shape((count, 16, 128))], 2
    )(total, mine)
    new_turned = lax.all_gather(new_share, ("hi", "lo"), axis=0, tiled=True)
    arrived = lax.all_to_all(outgoing, GROUP, split_axis=0, concat_axis=0, tiled=True)
    joined = call(join_kernel, shape((share, length)), 1, scratch=[pltpu.VMEM((share, length), F32)])(arrived)
    own = lax.all_gather(joined, "hi", axis=0, tiled=True)
    factor = 0.2 * max(length, cols) ** 0.5
    owned, packed = call(
        functools.partial(orthogonal_kernel, count, factor),
        [shape((cols, length)), shape((count, rows - 8, third + 32))],
        3,
        scalars=1,
        scratch=[pltpu.VMEM((cols, length), BF16)],
        flops=4 * ITERS * length * cols * cols,
    )(lo, *with_neighbours(own))
    packed, new_turned = lax.optimization_barrier((packed, new_turned))
    returned = lax.all_to_all(packed, GROUP, split_axis=0, concat_axis=0, tiled=True)
    new_momentum = call(
        functools.partial(unturn_kernel, share),
        shape((count, rows, cols)),
        1,
        scalars=1,
        scratch=by_slot,
        flops=2 * length * cols * cols,
    )(owner, new_turned)
    update = call(unpack_kernel, shape((count, rows, cols)), 3, scalars=2)(owner, lo, *with_neighbours(returned))
    return (new_momentum, update, owned.T[None])


def solution(mesh):
    reps, fsdp, sub = mesh.devices.shape
    mesh = Mesh(mesh.devices.reshape(reps // NEAR, NEAR, fsdp, sub), ("hi", "lo") + GROUP)
    return jax.shard_map(
        body,
        mesh=mesh,
        in_specs=(P(("hi", "lo"), None, GROUP, None), P(None, GROUP, None), P()),
        out_specs=(P(None, GROUP, None), P(None, GROUP, None), P(GROUP, None, None)),
        check_vma=False,
    )
```

```python
import functools

import jax
import jax.numpy as jnp
from jax import lax
from jax.experimental import pallas as pl
from jax.experimental.pallas import tpu as pltpu
from jax.sharding import Mesh, PartitionSpec as P

ITERS = 3
GROUP = ("fsdp", "sub")
F32 = jnp.float32
BF16 = jnp.bfloat16
SLOTS_PER_STEP = 16
LANES = 128
SPARE = 16
NEAR = 3
VMEM_LIMIT = 32 * 1024 * 1024
SMEM = pl.BlockSpec(memory_space=pltpu.SMEM)
VMEM = pl.BlockSpec(memory_space=pltpu.VMEM)


def call(kernel, out_shape, n_in, scalars=0, scratch=(), flops=0, moved=4 << 20):
    several = isinstance(out_shape, (list, tuple))
    return pl.pallas_call(
        kernel,
        out_shape=out_shape,
        in_specs=[SMEM] * scalars + [VMEM] * n_in,
        out_specs=[VMEM] * len(out_shape) if several else VMEM,
        scratch_shapes=list(scratch),
        compiler_params=pltpu.CompilerParams(vmem_limit_bytes=VMEM_LIMIT),
        cost_estimate=pl.CostEstimate(flops=flops, bytes_accessed=moved, transcendentals=0),
    )


def shape(dims, dtype=BF16):
    return jax.ShapeDtypeStruct(dims, dtype)


def each(count, one, together=8):
    together = min(together, count)

    def several(k, carry):
        for i in range(together):
            one(k * together + i)
        return carry

    lax.fori_loop(0, count // together, several, 0)


def select_rows(first, count, width):
    row = lax.broadcasted_iota(jnp.int32, (count, width), 0)
    col = lax.broadcasted_iota(jnp.int32, (count, width), 1)
    return (col == row + first).astype(BF16)


def select_shares(share, width):
    row = lax.broadcasted_iota(jnp.int32, (width, width), 0)
    col = lax.broadcasted_iota(jnp.int32, (width, width), 1)
    reps = width // share
    picked = row
    for r in range(reps):
        hi, lo = r // NEAR, r % NEAR
        start = lo * (width // NEAR) + hi * share
        inside = (row >= r * share) & (row < (r + 1) * share)
        picked = jnp.where(inside, row + (start - r * share), picked)
    return (col == picked).astype(BF16)


def place_by_owner(owner_ref, x_ref, by_slot):
    def place(j):
        by_slot[owner_ref[j]] = x_ref[j].astype(F32)

    each(x_ref.shape[0], place)


def turned_part(pick, by_slot, k, step):
    _, rows, cols = by_slot.shape
    part = by_slot[k * step : (k + 1) * step].reshape(step * rows, cols).astype(BF16)
    return lax.dot_general(pick, part, (((1,), (1,)), ((), ())), preferred_element_type=F32)


def turn_grads_kernel(share, x_ref_owner, x_ref, out_ref, by_slot):
    count, rows, cols = x_ref.shape
    place_by_owner(x_ref_owner, x_ref, by_slot)
    pick = select_shares(share, cols)
    step = min(2 * SLOTS_PER_STEP, count)
    tiles = step * rows // LANES
    held = share * count * rows // LANES
    out_ref[...] = jnp.zeros(out_ref.shape, BF16)
    for k in range(count // step):
        turned = turned_part(pick, by_slot, k, step)
        for r in range(cols // share):
            mine = turned[r * share : (r + 1) * share]
            block = jnp.concatenate([mine[:, t * LANES : (t + 1) * LANES] for t in range(tiles)], axis=0)
            first = r * (held + SPARE) + k * tiles * share
            out_ref[first : first + tiles * share] = block.astype(BF16)


def turn_share_kernel(owner_ref, first_ref, x_ref, out_ref, by_slot):
    count, rows, cols = x_ref.shape
    place_by_owner(owner_ref, x_ref, by_slot)
    pick = select_rows(first_ref[0], out_ref.shape[0], cols)
    step = SLOTS_PER_STEP
    for k in range(count // step):
        out_ref[:, k * step * rows : (k + 1) * step * rows] = turned_part(pick, by_slot, k, step).astype(BF16)


def moment_kernel(count, total_ref, momentum_ref, new_ref, out_ref):
    rows_of = momentum_ref.shape[0]
    held = total_ref[...].astype(F32)
    total = jnp.concatenate([held[t : t + rows_of] for t in range(0, held.shape[0], rows_of)], axis=1)
    moment = 0.95 * momentum_ref[...].astype(F32) + total
    new_ref[...] = moment.astype(BF16)
    ahead = total + 0.95 * moment
    rows = total.shape[1] // count
    for s in range(count):
        block = ahead[:, s * rows : (s + 1) * rows].astype(BF16)
        out_ref[s, :, :rows] = block[:16]
        out_ref[s, :8, 64 : 64 + rows] = block[16:]


def join_kernel(x_ref, out_ref, whole):
    count = x_ref.shape[0]
    rows = out_ref.shape[1] // count
    for s in range(count):
        block = x_ref[s].astype(F32)
        whole[:16, s * rows : (s + 1) * rows] = block[:, :rows]
        whole[16:, s * rows : (s + 1) * rows] = block[:8, 64 : 64 + rows]
    out_ref[...] = whole[...].astype(BF16)


def untransposed(part, eye):
    return lax.dot_general(part, eye, (((0,), (0,)), ((), ())), preferred_element_type=F32)


def next_y(old, product):
    return (3.4445 * old.astype(F32) + product).astype(BF16)


def orthogonal_kernel(count, factor, third_ref, own_ref, before_ref, after_ref, packed_ref, y_ref, mixed_ref):
    third, length = own_ref.shape
    lo = third_ref[0]

    def of_third(which):
        return pl.ds(pl.multiple_of(lax.rem(which, NEAR) * third, third), third)

    y_ref[of_third(lo), :] = own_ref[...]
    y_ref[of_third(lo + NEAR - 1), :] = before_ref[...]
    y_ref[of_third(lo + 1), :] = after_ref[...]
    squares = jnp.zeros((1, 1), F32)
    for k in range(NEAR):
        value = y_ref[k * third : (k + 1) * third, :].astype(F32)
        squares += jnp.sum(value * value, keepdims=True)
    inverse = 1.0 / (jnp.sqrt(squares) + 1e-07)
    for k in range(NEAR):
        at = slice(k * third, (k + 1) * third)
        y_ref[at, :] = (y_ref[at, :].astype(F32) * inverse).astype(BF16)
    rows = length // count
    step = SLOTS_PER_STEP
    for it in range(ITERS):
        y = y_ref[...]
        gram = lax.dot_general(y, y, (((1,), (1,)), ((), ())), preferred_element_type=F32).astype(BF16)
        square = jnp.dot(gram, gram, preferred_element_type=F32)
        mixed = (-4.775 * gram.astype(F32) + 2.0315 * square).astype(BF16)
        if it == ITERS - 1:
            break
        for k in range(count // step):
            at = slice(k * step * rows, (k + 1) * step * rows)
            y_ref[:, at] = next_y(y_ref[:, at], jnp.dot(mixed, y_ref[:, at], preferred_element_type=F32))
    mixed_ref[...] = mixed
    mine = mixed_ref[of_third(lo), :]
    eye = select_rows(0, third, third)
    top = rows - 8
    for k in range(count // step):
        at = slice(k * step * rows, (k + 1) * step * rows)
        new = next_y(y_ref[of_third(lo), at], jnp.dot(mine, y_ref[:, at], preferred_element_type=F32))
        update = untransposed((factor * new.astype(F32)).astype(BF16), eye).reshape(step, rows, third)
        low = [update[:, top:, 32 * j : 32 * j + 32] for j in range(third // 32)]
        low.append(jnp.zeros((step, top - 8 * len(low), 32), F32))
        block = jnp.concatenate([update[:, :top], jnp.concatenate(low, axis=1)], axis=2)
        packed_ref[k * step : (k + 1) * step] = block.astype(BF16)


def owned_kernel(count, factor, y_ref, mixed_ref, owned_ref):
    width = SLOTS_PER_STEP * y_ref.shape[1] // count
    for k in range(y_ref.shape[1] // width):
        at = slice(k * width, (k + 1) * width)
        new = next_y(y_ref[:, at], jnp.dot(mixed_ref[...], y_ref[:, at], preferred_element_type=F32))
        owned_ref[:, at] = (factor * new.astype(F32)).astype(BF16)


def unpack_kernel(owner_ref, third_ref, own_ref, before_ref, after_ref, out_ref):
    count, rows, cols = out_ref.shape
    start = pl.program_id(0) * count
    third = cols // NEAR
    top = rows - 8

    def columns(block):
        low = [block[8 * k : 8 * k + 8, third:] for k in range(third // 32)]
        return jnp.concatenate([block[:top, :third], jnp.concatenate(low, axis=1)], axis=0)

    for lo in range(NEAR):

        @pl.when(third_ref[0] == lo)
        def _():
            refs = [None] * NEAR
            refs[lo], refs[(lo + NEAR - 1) % NEAR], refs[(lo + 1) % NEAR] = own_ref, before_ref, after_ref

            def one(j):
                slot = owner_ref[start + j]
                parts = [columns(ref[slot].astype(F32)) for ref in refs]
                out_ref[j] = jnp.concatenate(parts, axis=1).astype(BF16)

            each(count, one, 4)


def unpack(owner, lo, own, before, after, out):
    count, rows, cols = out.shape
    together = min(SLOTS_PER_STEP, count)
    whole = pl.BlockSpec(own.shape, lambda k: (0, 0, 0))
    return pl.pallas_call(
        unpack_kernel,
        out_shape=out,
        grid=(count // together,),
        in_specs=[SMEM, SMEM, whole, whole, whole],
        out_specs=pl.BlockSpec((together, rows, cols), lambda k: (k, 0, 0)),
        compiler_params=pltpu.CompilerParams(vmem_limit_bytes=VMEM_LIMIT),
        cost_estimate=pl.CostEstimate(flops=0, bytes_accessed=4 << 20, transcendentals=0),
    )(owner, lo, own, before, after)


def unturn_kernel(share, owner_ref, x_ref, out_ref, by_slot):
    count, rows, cols = out_ref.shape
    step = SLOTS_PER_STEP
    pick = select_shares(share, cols)
    for k in range(count // step):
        part = untransposed(x_ref[:, k * step * rows : (k + 1) * step * rows], pick)
        by_slot[k * step : (k + 1) * step] = part.reshape(step, rows, cols)

    def one(j):
        out_ref[j] = by_slot[owner_ref[j]].astype(BF16)

    each(count, one)


def with_neighbours(part):
    reps = lax.axis_size("hi") * lax.axis_size("lo")
    before = lax.ppermute(part, ("hi", "lo"), [(r, (r + 1) % reps) for r in range(reps)])
    after = lax.ppermute(part, ("hi", "lo"), [((r + 1) % reps, r) for r in range(reps)])
    return part, before, after


def body(grads, momentum, owner):
    _, count, rows, cols = grads.shape
    reps = lax.axis_size("hi") * lax.axis_size("lo")
    share = cols // reps
    third = cols // NEAR
    length = count * rows
    hi, lo = lax.axis_index("hi").astype(jnp.int32), lax.axis_index("lo").astype(jnp.int32)
    first = (lo * third + hi * share).reshape(1)
    lo = lo.reshape(1)
    by_slot = [pltpu.VMEM((count, rows, cols), F32)]
    held = share * length // LANES
    turned = call(
        functools.partial(turn_grads_kernel, share),
        shape((reps * (held + SPARE - 1), LANES)),
        1,
        scalars=1,
        scratch=by_slot,
        flops=2 * length * cols * cols,
    )(owner, grads[0])
    total = lax.psum_scatter(turned, ("hi", "lo"), scatter_dimension=0, tiled=True)
    total = lax.optimization_barrier(total)
    total = lax.dynamic_slice(total, (lax.axis_index(("hi", "lo")), 0), (held, LANES))
    mine = call(
        turn_share_kernel, shape((share, length)), 1, scalars=2, scratch=by_slot, flops=2 * length * cols * share
    )(owner, first, momentum)
    new_share, outgoing = call(
        functools.partial(moment_kernel, count), [shape((share, length)), shape((count, 16, 128))], 2
    )(total, mine)
    arrived = lax.all_to_all(outgoing, GROUP, split_axis=0, concat_axis=0, tiled=True)
    joined = call(join_kernel, shape((share, length)), 1, scratch=[pltpu.VMEM((share, length), F32)])(arrived)
    own = lax.all_gather(joined, "hi", axis=0, tiled=True)
    own, before, after = with_neighbours(own)
    own, before, after, new_share = lax.optimization_barrier((own, before, after, new_share))
    new_turned = lax.all_gather(new_share, ("hi", "lo"), axis=0, tiled=True)
    factor = 0.2 * max(length, cols) ** 0.5
    packed, last, mixed = call(
        functools.partial(orthogonal_kernel, count, factor),
        [shape((count, rows - 8, third + 32)), shape((cols, length)), shape((cols, cols))],
        3,
        scalars=1,
        flops=4 * ITERS * length * cols * cols,
    )(lo, own, before, after)
    returned = lax.all_to_all(packed, GROUP, split_axis=0, concat_axis=0, tiled=True)
    returned = with_neighbours(returned)
    owned = call(
        functools.partial(owned_kernel, count, factor), shape((cols, length)), 2, flops=2 * length * cols * cols
    )(last, mixed)
    new_turned, owned = lax.optimization_barrier((new_turned, owned))
    new_momentum = call(
        functools.partial(unturn_kernel, share),
        shape((count, rows, cols)),
        1,
        scalars=1,
        scratch=by_slot,
        flops=2 * length * cols * cols,
    )(owner, new_turned)
    *returned, new_momentum = lax.optimization_barrier((*returned, new_momentum))
    update = unpack(owner, lo, *returned, shape((count, rows, cols)))
    return (new_momentum, update, owned.T[None])


def solution(mesh):
    reps, fsdp, sub = mesh.devices.shape
    mesh = Mesh(mesh.devices.reshape(reps // NEAR, NEAR, fsdp, sub), ("hi", "lo") + GROUP)
    return jax.shard_map(
        body,
        mesh=mesh,
        in_specs=(P(("hi", "lo"), None, GROUP, None), P(None, GROUP, None), P()),
        out_specs=(P(None, GROUP, None), P(None, GROUP, None), P(GROUP, None, None)),
        check_vma=False,
    )
```

```python
import functools

import jax
import jax.numpy as jnp
from jax import lax
from jax.experimental import pallas as pl
from jax.experimental.pallas import tpu as pltpu
from jax.sharding import Mesh, PartitionSpec as P

ITERS = 3
GROUP = ("fsdp", "sub")
F32 = jnp.float32
BF16 = jnp.bfloat16
SLOTS_PER_STEP = 16
LANES = 128
SPARE = 16
NEAR = 3
VMEM_LIMIT = 20 * 1024 * 1024
SMEM = pl.BlockSpec(memory_space=pltpu.SMEM)
VMEM = pl.BlockSpec(memory_space=pltpu.VMEM)


def call(kernel, out_shape, n_in, scalars=0, scratch=(), flops=0, moved=4 << 20):
    several = isinstance(out_shape, (list, tuple))
    return pl.pallas_call(
        kernel,
        out_shape=out_shape,
        in_specs=[SMEM] * scalars + [VMEM] * n_in,
        out_specs=[VMEM] * len(out_shape) if several else VMEM,
        scratch_shapes=list(scratch),
        compiler_params=pltpu.CompilerParams(vmem_limit_bytes=VMEM_LIMIT),
        cost_estimate=pl.CostEstimate(flops=flops, bytes_accessed=moved, transcendentals=0),
    )


def shape(dims, dtype=BF16):
    return jax.ShapeDtypeStruct(dims, dtype)


def each(count, one, together=8):
    together = min(together, count)

    def several(k, carry):
        for i in range(together):
            one(k * together + i)
        return carry

    lax.fori_loop(0, count // together, several, 0)


def select_rows(first, count, width):
    row = lax.broadcasted_iota(jnp.int32, (count, width), 0)
    col = lax.broadcasted_iota(jnp.int32, (count, width), 1)
    return (col == row + first).astype(BF16)


def select_shares(share, width):
    row = lax.broadcasted_iota(jnp.int32, (width, width), 0)
    col = lax.broadcasted_iota(jnp.int32, (width, width), 1)
    reps = width // share
    picked = row
    for r in range(reps):
        hi, lo = r // NEAR, r % NEAR
        start = lo * (width // NEAR) + hi * share
        inside = (row >= r * share) & (row < (r + 1) * share)
        picked = jnp.where(inside, row + (start - r * share), picked)
    return (col == picked).astype(BF16)


def place_by_owner(owner_ref, x_ref, by_slot):
    def place(j):
        by_slot[owner_ref[j]] = x_ref[j].astype(F32)

    each(x_ref.shape[0], place)


def turned_part(pick, by_slot, k, step):
    _, rows, cols = by_slot.shape
    part = by_slot[k * step : (k + 1) * step].reshape(step * rows, cols).astype(BF16)
    return lax.dot_general(pick, part, (((1,), (1,)), ((), ())), preferred_element_type=F32)


def turn_grads_kernel(share, x_ref_owner, x_ref, out_ref, by_slot):
    count, rows, cols = x_ref.shape
    place_by_owner(x_ref_owner, x_ref, by_slot)
    pick = select_shares(share, cols)
    step = min(2 * SLOTS_PER_STEP, count)
    tiles = step * rows // LANES
    held = share * count * rows // LANES
    for r in range(cols // share):
        after = slice(r * (held + SPARE) + held, min((r + 1) * (held + SPARE), out_ref.shape[0]))
        out_ref[after] = jnp.zeros((after.stop - after.start, LANES), BF16)
    for k in range(count // step):
        turned = turned_part(pick, by_slot, k, step)
        for r in range(cols // share):
            mine = turned[r * share : (r + 1) * share]
            block = jnp.concatenate([mine[:, t * LANES : (t + 1) * LANES] for t in range(tiles)], axis=0)
            first = r * (held + SPARE) + k * tiles * share
            out_ref[first : first + tiles * share] = block.astype(BF16)


def turn_share_kernel(owner_ref, first_ref, x_ref, out_ref, by_slot):
    count, rows, cols = x_ref.shape
    place_by_owner(owner_ref, x_ref, by_slot)
    pick = select_rows(first_ref[0], out_ref.shape[0], cols)
    step = SLOTS_PER_STEP
    for k in range(count // step):
        out_ref[:, k * step * rows : (k + 1) * step * rows] = turned_part(pick, by_slot, k, step).astype(BF16)


def moment_kernel(count, total_ref, momentum_ref, new_ref, out_ref):
    rows_of = momentum_ref.shape[0]
    held = total_ref[...].astype(F32)
    total = jnp.concatenate([held[t : t + rows_of] for t in range(0, held.shape[0], rows_of)], axis=1)
    moment = 0.95 * momentum_ref[...].astype(F32) + total
    new_ref[...] = moment.astype(BF16)
    ahead = total + 0.95 * moment
    rows = total.shape[1] // count
    for s in range(count):
        block = ahead[:, s * rows : (s + 1) * rows].astype(BF16)
        out_ref[s, :, :rows] = block[:16]
        out_ref[s, :8, 64 : 64 + rows] = block[16:]


def join_kernel(x_ref, out_ref, whole):
    count = x_ref.shape[0]
    rows = out_ref.shape[1] // count
    for s in range(count):
        block = x_ref[s].astype(F32)
        whole[:16, s * rows : (s + 1) * rows] = block[:, :rows]
        whole[16:, s * rows : (s + 1) * rows] = block[:8, 64 : 64 + rows]
    out_ref[...] = whole[...].astype(BF16)


def untransposed(part, eye):
    return lax.dot_general(part, eye, (((0,), (0,)), ((), ())), preferred_element_type=F32)


def next_y(old, product):
    return (3.4445 * old.astype(F32) + product).astype(BF16)


def orthogonal_kernel(count, factor, third_ref, own_ref, before_ref, after_ref, packed_ref, y_ref, mixed_ref):
    third, length = own_ref.shape
    lo = third_ref[0]

    def of_third(which):
        return pl.ds(pl.multiple_of(lax.rem(which, NEAR) * third, third), third)

    y_ref[of_third(lo), :] = own_ref[...]
    y_ref[of_third(lo + NEAR - 1), :] = before_ref[...]
    y_ref[of_third(lo + 1), :] = after_ref[...]
    squares = jnp.zeros((1, 1), F32)
    for k in range(NEAR):
        value = y_ref[k * third : (k + 1) * third, :].astype(F32)
        squares += jnp.sum(value * value, keepdims=True)
    inverse = 1.0 / (jnp.sqrt(squares) + 1e-07)
    for k in range(NEAR):
        at = slice(k * third, (k + 1) * third)
        y_ref[at, :] = (y_ref[at, :].astype(F32) * inverse).astype(BF16)
    rows = length // count
    step = SLOTS_PER_STEP
    for it in range(ITERS):
        y = y_ref[...]
        gram = lax.dot_general(y, y, (((1,), (1,)), ((), ())), preferred_element_type=F32).astype(BF16)
        square = jnp.dot(gram, gram, preferred_element_type=F32)
        mixed = (-4.775 * gram.astype(F32) + 2.0315 * square).astype(BF16)
        if it == ITERS - 1:
            break
        for k in range(count // step):
            at = slice(k * step * rows, (k + 1) * step * rows)
            y_ref[:, at] = next_y(y_ref[:, at], jnp.dot(mixed, y_ref[:, at], preferred_element_type=F32))
    mixed_ref[...] = mixed
    mine = mixed_ref[of_third(lo), :]
    eye = select_rows(0, third, third)
    top = rows - 8
    for k in range(count // step):
        at = slice(k * step * rows, (k + 1) * step * rows)
        new = next_y(y_ref[of_third(lo), at], jnp.dot(mine, y_ref[:, at], preferred_element_type=F32))
        update = untransposed((factor * new.astype(F32)).astype(BF16), eye).reshape(step, rows, third)
        low = [update[:, top:, 32 * j : 32 * j + 32] for j in range(third // 32)]
        low.append(jnp.zeros((step, top - 8 * len(low), 32), F32))
        block = jnp.concatenate([update[:, :top], jnp.concatenate(low, axis=1)], axis=2)
        packed_ref[k * step : (k + 1) * step] = block.astype(BF16)


def owned_kernel(count, factor, y_ref, mixed_ref, owned_ref):
    width = SLOTS_PER_STEP * y_ref.shape[1] // count
    for k in range(y_ref.shape[1] // width):
        at = slice(k * width, (k + 1) * width)
        new = next_y(y_ref[:, at], jnp.dot(mixed_ref[...], y_ref[:, at], preferred_element_type=F32))
        owned_ref[:, at] = (factor * new.astype(F32)).astype(BF16)


def unpack_kernel(owner_ref, third_ref, own_ref, before_ref, after_ref, out_ref):
    count, rows, cols = out_ref.shape
    start = pl.program_id(0) * count
    third = cols // NEAR
    top = rows - 8

    def columns(block):
        low = [block[8 * k : 8 * k + 8, third:] for k in range(third // 32)]
        return jnp.concatenate([block[:top, :third], jnp.concatenate(low, axis=1)], axis=0)

    for lo in range(NEAR):

        @pl.when(third_ref[0] == lo)
        def _():
            refs = [None] * NEAR
            refs[lo], refs[(lo + NEAR - 1) % NEAR], refs[(lo + 1) % NEAR] = own_ref, before_ref, after_ref

            def one(j):
                slot = owner_ref[start + j]
                parts = [columns(ref[slot].astype(F32)) for ref in refs]
                out_ref[j] = jnp.concatenate(parts, axis=1).astype(BF16)

            each(count, one, 4)


def unpack(owner, lo, own, before, after, out):
    count, rows, cols = out.shape
    together = min(SLOTS_PER_STEP, count)
    whole = pl.BlockSpec(own.shape, lambda k: (0, 0, 0))
    return pl.pallas_call(
        unpack_kernel,
        out_shape=out,
        grid=(count // together,),
        in_specs=[SMEM, SMEM, whole, whole, whole],
        out_specs=pl.BlockSpec((together, rows, cols), lambda k: (k, 0, 0)),
        compiler_params=pltpu.CompilerParams(vmem_limit_bytes=VMEM_LIMIT),
        cost_estimate=pl.CostEstimate(flops=0, bytes_accessed=4 << 20, transcendentals=0),
    )(owner, lo, own, before, after)


def unturn_kernel(share, owner_ref, x_ref, out_ref, by_slot):
    count, rows, cols = out_ref.shape
    step = SLOTS_PER_STEP
    pick = select_shares(share, cols)
    for k in range(count // step):
        part = untransposed(x_ref[:, k * step * rows : (k + 1) * step * rows], pick)
        by_slot[k * step : (k + 1) * step] = part.reshape(step, rows, cols)

    def one(j):
        out_ref[j] = by_slot[owner_ref[j]].astype(BF16)

    each(count, one)


def with_neighbours(part):
    reps = lax.axis_size("hi") * lax.axis_size("lo")
    before = lax.ppermute(part, ("hi", "lo"), [(r, (r + 1) % reps) for r in range(reps)])
    after = lax.ppermute(part, ("hi", "lo"), [((r + 1) % reps, r) for r in range(reps)])
    return part, before, after


def body(grads, momentum, owner):
    _, count, rows, cols = grads.shape
    reps = lax.axis_size("hi") * lax.axis_size("lo")
    share = cols // reps
    third = cols // NEAR
    length = count * rows
    hi, lo = lax.axis_index("hi").astype(jnp.int32), lax.axis_index("lo").astype(jnp.int32)
    first = (lo * third + hi * share).reshape(1)
    lo = lo.reshape(1)
    by_slot = [pltpu.VMEM((count, rows, cols), F32)]
    held = share * length // LANES
    turned = call(
        functools.partial(turn_grads_kernel, share),
        shape((reps * (held + SPARE - 1), LANES)),
        1,
        scalars=1,
        scratch=by_slot,
        flops=2 * length * cols * cols,
    )(owner, grads[0])
    total = lax.psum_scatter(turned, ("hi", "lo"), scatter_dimension=0, tiled=True)
    total = lax.optimization_barrier(total)
    total = lax.dynamic_slice(total, (lax.axis_index(("hi", "lo")), 0), (held, LANES))
    mine = call(
        turn_share_kernel, shape((share, length)), 1, scalars=2, scratch=by_slot, flops=2 * length * cols * share
    )(owner, first, momentum)
    new_share, outgoing = call(
        functools.partial(moment_kernel, count), [shape((share, length)), shape((count, 16, 128))], 2
    )(total, mine)
    arrived = lax.all_to_all(outgoing, GROUP, split_axis=0, concat_axis=0, tiled=True)
    joined = call(join_kernel, shape((share, length)), 1, scratch=[pltpu.VMEM((share, length), F32)])(arrived)
    own = lax.all_gather(joined, "hi", axis=0, tiled=True)
    own, before, after = with_neighbours(own)
    own, before, after, new_share = lax.optimization_barrier((own, before, after, new_share))
    new_turned = lax.all_gather(new_share, ("hi", "lo"), axis=0, tiled=True)
    factor = 0.2 * max(length, cols) ** 0.5
    packed, last, mixed = call(
        functools.partial(orthogonal_kernel, count, factor),
        [shape((count, rows - 8, third + 32)), shape((cols, length)), shape((cols, cols))],
        3,
        scalars=1,
        flops=4 * ITERS * length * cols * cols,
    )(lo, own, before, after)
    returned = lax.all_to_all(packed, GROUP, split_axis=0, concat_axis=0, tiled=True)
    returned = with_neighbours(returned)
    owned = call(
        functools.partial(owned_kernel, count, factor), shape((cols, length)), 2, flops=2 * length * cols * cols
    )(last, mixed)
    new_turned, owned = lax.optimization_barrier((new_turned, owned))
    new_momentum = call(
        functools.partial(unturn_kernel, share),
        shape((count, rows, cols)),
        1,
        scalars=1,
        scratch=by_slot,
        flops=2 * length * cols * cols,
    )(owner, new_turned)
    *returned, new_momentum = lax.optimization_barrier((*returned, new_momentum))
    update = unpack(owner, lo, *returned, shape((count, rows, cols)))
    return (new_momentum, update, owned.T[None])


def solution(mesh):
    reps, fsdp, sub = mesh.devices.shape
    mesh = Mesh(mesh.devices.reshape(reps // NEAR, NEAR, fsdp, sub), ("hi", "lo") + GROUP)
    return jax.shard_map(
        body,
        mesh=mesh,
        in_specs=(P(("hi", "lo"), None, GROUP, None), P(None, GROUP, None), P()),
        out_specs=(P(None, GROUP, None), P(None, GROUP, None), P(GROUP, None, None)),
        check_vma=False,
    )
```
